32 devices in a mesh: groups: 2 (over y), slab: 4 (over z), radar: 4 (over x, core).
Axes of the slice: x: 2, y: 2, z: 4, core: 2. Of those that a mesh axis runs over, the one named last changes fastest.
Arguments:
- wind: float32 [8, 2048, 2, 2048], P(('groups', 'radar'), 'slab'), parts along dimension 0, may hold values from -6 to 6
- obs_velocity: float32 [16384, 128], P(('groups', 'slab', 'radar')), parts along dimension 0, may hold values from -6 to 6
- gate_weight: float32 [16384, 128], P(('groups', 'slab', 'radar')), parts along dimension 0, may hold values from 0.1 to 1
- azimuth: float32 [16384, 128], P(('groups', 'slab', 'radar')), parts along dimension 0, may hold values from -3.140625 to 3.140625
- block_owner: int32 [16384, 1], P(('groups', 'slab', 'radar')), parts along dimension 0, may hold values from 0 to 3; in each aligned block of 512 rows (0 to 511, 512 to 1023, ...) at most 256 rows name the same one
- block_cell: int32 [16384], P(('groups', 'slab', 'radar')), parts along dimension 0, may hold values from 0 to 1048575
Outputs:
- updated_wind: float32 [8, 2048, 2, 2048], P(('groups', 'radar'), 'slab'), parts along dimension 0
- total_cost: float32 [2], P('groups'), parts along dimension 0
The draws below stay inside these ranges and needn't reach their ends.
There are 2 independent parts, one for each index of `groups`. The reference program is written for one: setup_inputs(seed, part) draws one part's arguments, and reference() takes and returns one part's arrays. A program takes and returns all parts, laid end to end along the dimension named above; each array names one. Nothing has to cross between parts.
Inputs may be any that keep to these rules, and one draw needn't show every extreme that they name: `block_owner`: among the 512 blocks of one device at most 256 name the same owner, and in every draw some owner is named by exactly 256 of them.
All inputs are finite; a program needn't handle non-finite values.
Results may differ from the reference program's by a relative error of at most 0.0017.
The reference program's roundings to bfloat16 on the way count: a program that leaves them out, or rounds other values in their place, can miss the bound.
Values may be sent and summed in bfloat16 or wider, within the bound.
A program may use at most 128 MiB of HBM per device.

```python
import math
import jax
import jax.numpy as jnp
import numpy as np
from jax import lax

NX = 2048
NY = 2048
GATES = 128
NB = 512
CX = 512
CAP = 256
LEVELS = 4
BLOCKS = 8192
N_SLAB = 4


def plant(values, key, smallest, high):
    index_at = [jax.random.randint(jax.random.fold_in(key, axis), (), 0, length) for axis, length in enumerate(values.shape)]
    widest = values.shape.index(max(values.shape))
    next_to = index_at[:widest] + [(index_at[widest] + 1) % values.shape[widest]] + index_at[widest + 1:]
    return values.at[tuple(index_at)].set(smallest).at[tuple(next_to)].set(high)


def steps_of(own_key, shape, split, low, top_value):
    def one(position, parts):
        heights = jax.random.uniform(jax.random.fold_in(jax.random.fold_in(own_key, 6), position), (parts,), jnp.float32, low / len(split), top_value / len(split))
        return jnp.repeat(jnp.exp(heights), shape[position] // parts).reshape((-1,) + (1,) * (len(shape) - position - 1))

    level = one(*split[0])
    for cut in split[1:]:
        level = level * one(*cut)
    return level


def deal_out(rng, own, number, rows, amount, top, most, lean):
    order = jax.random.permutation(rng, amount)
    crowded, common = load_shares(amount, rows * top, most, lean, True), load_shares(amount, rows * top, most, lean, False)
    places = jnp.arange(amount)

    def named(tallies, rotation):
        used = int((tallies > 0).sum())
        fixed = max(1, used // 4)
        moved = fixed + (places - fixed + rotation * (used - fixed)) % max(1, amount - fixed)
        return jnp.zeros((amount,), jnp.int32).at[order[jnp.where(places < fixed, places, moved)]].set(jnp.asarray(tallies, jnp.int32))

    tallies = jnp.where(number % 4 == 0, named(crowded, number // 4), named(common, number - number // 4 - 1))
    mixed = jax.random.permutation(jax.random.fold_in(own, 3), amount)
    source_of, taker = mixed[0:amount // 2 * 2:2], mixed[1:amount // 2 * 2:2]
    room = jnp.minimum(tallies[source_of] - 1, most - tallies[taker]) // 2
    room = jnp.where((source_of == order[0]) | (taker == order[0]) | (tallies[taker] == 0), 0, jnp.maximum(room, 0))
    moved = jax.random.randint(jax.random.fold_in(own, 4), (amount // 2,), 0, 1 << 20) % (room + 1)
    tallies = tallies.at[source_of].add(-moved).at[taker].add(moved)
    labels = jnp.searchsorted(jnp.cumsum(tallies), jnp.arange(rows * top), side="right").astype(jnp.int32)
    listing = labels.reshape(top, rows).T
    listing = listing[jax.random.permutation(jax.random.fold_in(own, 1), rows)]
    rotation = jax.random.randint(jax.random.fold_in(own, 2), (rows, 1), 0, top)
    return jnp.take_along_axis(listing, (jnp.arange(top)[None, :] + rotation) % top, axis=1)


def load_shares(count, total, most, slope, full):
    weights = [(1 << 20) // math.isqrt(standing ** slope) + 1 for standing in range(1, count + 1)]
    largest = most if full else min(most, max(-(-total // count), total * weights[0] // sum(weights)))
    least = 1 if total - largest >= count - 1 else 0
    given, spare = [largest] + [least] * (count - 1), total - largest - least * (count - 1)
    while spare > 0:
        candidates = [i for i in range(1, count) if given[i] < largest] or [i for i in range(1, count) if given[i] < most]
        whole, remaining = sum([weights[i] for i in candidates]), spare
        for i in candidates:
            more = min(most - given[i], max(1, remaining * weights[i] // whole), spare)
            given[i] = given[i] + more
            spare = spare - more
    return np.array(given)


def gaussian(key, extent, width, limit, pieces=(), kind=jnp.bfloat16):
    drawn = width * jax.random.normal(key, extent, jnp.float32)
    if pieces:
        drawn = drawn * steps_of(key, extent, pieces, -0.22, 0.18)
    return jnp.clip(drawn, -limit, limit).astype(kind)


def setup_inputs(seed: int = 0, part: int = 0) -> dict:
    key_of = jax.random.split(jax.random.key(seed), 7)
    part_keys = jax.random.split(jax.random.fold_in(key_of[6], part), 7)
    wind = gaussian(part_keys[0], (LEVELS, NX, 2, NY), 1.0, 6.0, ((0, 4), (1, 4)), jnp.float32)
    obs_velocity = gaussian(part_keys[1], (BLOCKS, GATES), 1.0, 6.0, ((0, 16),), jnp.float32)
    gate_weight = jnp.clip(jnp.exp(math.log(1.0) - 2.3025851 * jax.random.uniform(part_keys[2], (BLOCKS, GATES), jnp.float32) ** steps_of(part_keys[2], (BLOCKS, GATES), ((0, 16),), -0.2, 0.2)), 0.1, 1.0)
    azimuth = jnp.clip(jax.random.uniform(part_keys[3], (BLOCKS, GATES), jnp.float32, -3.140625, 3.140625), -3.140625, 3.140625)
    block_owner_keys = jax.random.split(jax.random.fold_in(part_keys[4], 1), BLOCKS // NB)
    block_owner_turns = jax.random.permutation(jax.random.fold_in(part_keys[4], 3), BLOCKS // NB)
    block_owner = jax.vmap(lambda own, number: deal_out(jax.random.fold_in(part_keys[4], 2), own, number, NB, N_SLAB, 1, CAP, 2))(block_owner_keys, block_owner_turns).reshape((BLOCKS, 1))
    block_cell = plant(jax.random.randint(part_keys[5], (BLOCKS,), 0, CX * NY), jax.random.fold_in(part_keys[5], 1), 0, (CX * NY) - 1).astype(jnp.int32)
    return {"wind": wind, "obs_velocity": obs_velocity, "gate_weight": gate_weight, "azimuth": azimuth, "block_owner": block_owner, "block_cell": block_cell}


divergence_weight = 2.0
spectral_shift = 0.0001

def dst_table(length):
    rows = jnp.arange(length, dtype=jnp.int32) + 1
    phase = rows[:, None] * rows[None, :] % (2 * (length + 1))
    angle = math.pi / (length + 1) * phase.astype(jnp.float32)
    return (math.sqrt(2.0 / (length + 1)) * jnp.sin(angle)).astype(jnp.bfloat16)

def eigen_values(length, start, count):
    waves = (start + jnp.arange(count, dtype=jnp.int32) + 1).astype(jnp.float32)
    return 4.0 * jnp.sin(math.pi / (2 * (length + 1)) * waves) ** 2

def reference(wind, obs_velocity, gate_weight, azimuth, block_owner, block_cell):
    blocks = obs_velocity.shape[0]
    ident = jnp.arange(blocks, dtype=jnp.int32)
    level = ident // NB % LEVELS
    column = block_owner[:, 0] * CX + block_cell // NY
    row_y = block_cell % NY
    u_val = wind[level, column, 0, row_y]
    v_val = wind[level, column, 1, row_y]
    cosine = jnp.cos(azimuth)
    sine = jnp.sin(azimuth)
    misfit = gate_weight * (cosine * u_val[:, None] + sine * v_val[:, None]) - obs_velocity
    cost_obs = 0.5 * jnp.sum(misfit * misfit)
    part_u = lax.optimization_barrier(jnp.sum(gate_weight * cosine * misfit, axis=1))
    part_v = lax.optimization_barrier(jnp.sum(gate_weight * sine * misfit, axis=1))
    grad_obs = jnp.zeros_like(wind).at[level, column, 0, row_y].add(part_u)
    grad_obs = grad_obs.at[level, column, 1, row_y].add(part_v)
    u_field = wind[:, :, 0, :]
    v_field = wind[:, :, 1, :]
    pad_u = jnp.pad(u_field, ((0, 0), (1, 1), (0, 0)))
    pad_v = jnp.pad(v_field, ((0, 0), (0, 0), (1, 1)))
    div = 0.5 * (pad_u[:, 2:] - pad_u[:, :-2]) + 0.5 * (pad_v[:, :, 2:] - pad_v[:, :, :-2])
    cost_div = 0.5 * divergence_weight * jnp.sum(div * div)
    total_cost = cost_obs + cost_div
    div_x = jnp.pad(div, ((0, 0), (1, 1), (0, 0)))
    div_y = jnp.pad(div, ((0, 0), (0, 0), (1, 1)))
    grad_u = divergence_weight * 0.5 * (div_x[:, :-2] - div_x[:, 2:])
    grad_v = divergence_weight * 0.5 * (div_y[:, :, :-2] - div_y[:, :, 2:])
    gradient = grad_obs + jnp.stack([grad_u, grad_v], axis=2)
    table_x = dst_table(NX).astype(jnp.float32)
    table_y = dst_table(NY).astype(jnp.float32)
    eig = eigen_values(NX, 0, NX)[:, None, None] + eigen_values(NY, 0, NY)[None, None, :] + spectral_shift
    high = lax.Precision.HIGHEST

    def one_level(field):
        low = field.astype(jnp.bfloat16).astype(jnp.float32)
        spec_y = jnp.einsum('xcy,yk->xck', low, table_y, precision=high).astype(jnp.bfloat16).astype(jnp.float32)
        spec = jnp.einsum('kx,xcy->kcy', table_x, spec_y, precision=high)
        scaled = spec / eig
        energy = jnp.sum(spec * scaled)
        lowered = scaled.astype(jnp.bfloat16).astype(jnp.float32)
        back_x = jnp.einsum('kx,xcy->kcy', table_x, lowered, precision=high).astype(jnp.bfloat16).astype(jnp.float32)
        precond = jnp.einsum('xck,ky->xcy', back_x, table_y, precision=high)
        return (precond, energy)
    precond, energies = lax.map(one_level, gradient)
    energy = jnp.sum(energies)
    updated_wind = wind - total_cost / energy * precond
    return (updated_wind, jnp.reshape(total_cost, (1,)))
```

```python
import functools
import math

import jax
import jax.numpy as jnp
from jax import lax
from jax.experimental import pallas as pl
from jax.experimental.pallas import tpu as pltpu
from jax.sharding import PartitionSpec as P

divergence_weight = 2.0
spectral_shift = 0.0001
vmem_bytes = 56 * 1024 * 1024
halo = 8


def dst_table(length):
    inner = math.gcd(length, 64)
    outer = length // inner
    waves = lax.iota(jnp.int32, length) + 1
    period = 2 * (length + 1)
    scale = math.sqrt(2.0 / (length + 1))

    def angles(steps):
        phase = steps[:, None] * waves[None, :] % period
        return math.pi / (length + 1) * phase.astype(jnp.float32)

    coarse = angles(lax.iota(jnp.int32, outer) * inner)
    fine = angles(lax.iota(jnp.int32, inner) + 1)
    coarse_s, coarse_c, fine_s, fine_c = lax.optimization_barrier(
        (scale * jnp.sin(coarse), scale * jnp.cos(coarse), jnp.sin(fine), jnp.cos(fine))
    )
    table = coarse_s[:, None, :] * fine_c[None] + coarse_c[:, None, :] * fine_s[None]
    return table.astype(jnp.bfloat16).reshape(length, length)


def eigen_values(length, start, count):
    waves = (start + lax.iota(jnp.int32, count) + 1).astype(jnp.float32)
    return 4.0 * jnp.sin(math.pi / (2 * (length + 1)) * waves) ** 2


def gradient_kernel(ends, cell_ref, coef_ref, wind_ref, out_ref, cost_ref, grad_ref, sum_ref):
    _, rows, width = out_ref.shape
    slabs, _, capacity = coef_ref.shape
    here = lax.axis_index("slab")
    step = min(32, rows)
    tall = step + 2 * halo

    sum_ref[...] = jnp.zeros_like(sum_ref)
    lane = lax.broadcasted_iota(jnp.int32, (tall, width), 1)
    row = lax.broadcasted_iota(jnp.int32, (tall, width), 0)

    def y_sides(field):
        before = jnp.where(lane == 0, 0.0, pltpu.roll(field, 1, 1))
        after = jnp.where(lane == width - 1, 0.0, pltpu.roll(field, width - 1, 1))
        return before, after

    def stencil(i, carry):
        start = pl.multiple_of(i * step, 8)
        u = wind_ref[0, pl.ds(start, tall), :]
        v = wind_ref[1, pl.ds(start, tall), :]
        before, after = y_sides(v)
        div = 0.5 * (pltpu.roll(u, tall - 1, 0) - pltpu.roll(u, 1, 0)) + 0.5 * (after - before)
        place = here * rows + start - halo + row
        div = jnp.where((place >= 0) & (place < ends), div, 0.0)
        kept = div[halo : halo + step]
        sum_ref[...] += jnp.sum((kept * kept).reshape(step // 8, 8, width), axis=0)
        grad_u = pltpu.roll(div, 1, 0) - pltpu.roll(div, tall - 1, 0)
        before, after = y_sides(div)
        grad_v = before - after
        scale = divergence_weight * 0.5
        grad_ref[0, pl.ds(start, step), :] = scale * grad_u[halo : halo + step]
        grad_ref[1, pl.ds(start, step), :] = scale * grad_v[halo : halo + step]
        return carry

    lax.fori_loop(0, rows // step, stencil, 0)

    spot = lax.broadcasted_iota(jnp.int32, (8, 128), 0) * 128
    spot = spot + lax.broadcasted_iota(jnp.int32, (8, 128), 1)

    def gate_block(s, i, total):
        cell = cell_ref[s, i]
        x = cell // width
        y = cell - x * width
        top = pl.multiple_of(x // 8 * 8, 8)
        first = pl.multiple_of(y // 128 * 128, 128)
        mask = spot == (x - top) * 128 + (y - first)
        u = wind_ref[0, pl.ds(pl.multiple_of(top + halo, 8), 8), pl.ds(first, 128)]
        v = wind_ref[1, pl.ds(pl.multiple_of(top + halo, 8), 8), pl.ds(first, 128)]
        uu, uv, vv = coef_ref[s, 0, i], coef_ref[s, 1, i], coef_ref[s, 2, i]
        ou, ov = coef_ref[s, 3, i], coef_ref[s, 4, i]
        part_u = uu * u + uv * v - ou
        part_v = uv * u + vv * v - ov
        grad_ref[0, pl.ds(top, 8), pl.ds(first, 128)] += jnp.where(mask, part_u, 0.0)
        grad_ref[1, pl.ds(top, 8), pl.ds(first, 128)] += jnp.where(mask, part_v, 0.0)
        return total + jnp.where(mask, u * (part_u - ou) + v * (part_v - ov), 0.0)

    def gate_group(t, total):
        s = t // (capacity // 8)
        base = (t - s * (capacity // 8)) * 8
        for k in range(8):
            total = gate_block(s, base + k, total)
        return total

    total = lax.fori_loop(
        0, slabs * capacity // 8, gate_group, jnp.zeros((8, 128), jnp.float32)
    )
    cost_div = 0.5 * divergence_weight * jnp.sum(sum_ref[...], keepdims=True)
    cost_ref[...] = cost_div + 0.5 * jnp.sum(total, keepdims=True)

    def lower(i, carry):
        at = pl.ds(pl.multiple_of(i * step, 16), step)
        out_ref[0, at, :] = grad_ref[0, at, :].astype(jnp.bfloat16)
        out_ref[1, at, :] = grad_ref[1, at, :].astype(jnp.bfloat16)
        return carry

    lax.fori_loop(0, rows // step, lower, 0)


def y_forward_kernel(grad_ref, table_ref, out_ref):
    parts, _, part = out_ref.shape
    spec = jnp.dot(grad_ref[0], table_ref[...], preferred_element_type=jnp.float32)
    spec = spec.astype(jnp.bfloat16)
    for d in range(parts):
        out_ref[d] = spec[:, d * part : (d + 1) * part]


def x_kernel(cols_ref, table_ref, lam_x_ref, lam_y_ref, out_ref, energy_ref, scaled_ref):
    phase, i = pl.program_id(0), pl.program_id(1)
    slabs, rows, part = cols_ref.shape
    block = table_ref.shape[0]

    @pl.when((phase == 0) & (i == 0))
    def _():
        energy_ref[...] = jnp.zeros_like(energy_ref)

    @pl.when(phase == 0)
    def _():
        cols = cols_ref[...].reshape(slabs * rows, part)
        spec = jnp.dot(table_ref[...], cols, preferred_element_type=jnp.float32)
        scaled = spec / (lam_x_ref[...] + lam_y_ref[...] + spectral_shift)
        energy_ref[...] += jnp.sum((spec * scaled).reshape(block // 8, 8, part), axis=0)
        scaled_ref[pl.ds(pl.multiple_of(i * block, block), block), :] = scaled.astype(jnp.bfloat16)

    @pl.when(phase == 1)
    def _():
        back = jnp.dot(table_ref[...], scaled_ref[...], preferred_element_type=jnp.float32)
        out_ref[...] = back.astype(jnp.bfloat16).reshape(out_ref.shape)


def y_back_kernel(rows_ref, table_ref, out_ref, held_ref):
    slabs, _, part = rows_ref.shape

    @pl.when(pl.program_id(0) == 0)
    def _():
        for d in range(slabs):
            held_ref[:, d * part : (d + 1) * part] = rows_ref[d]

    out_ref[...] = jnp.dot(held_ref[...], table_ref[...], preferred_element_type=jnp.float32)


def whole(shape):
    return pl.BlockSpec(shape, lambda *_: (0,) * len(shape))


def cost_of(flops, moved):
    return pl.CostEstimate(flops=flops, bytes_accessed=moved, transcendentals=0)


def params(steps):
    return pltpu.CompilerParams(
        vmem_limit_bytes=vmem_bytes, dimension_semantics=("arbitrary",) * steps
    )


def gradient_of(cells, coefs, wind_ext, rows, ends):
    _, tall, width = wind_ext.shape
    smem = pl.BlockSpec(memory_space=pltpu.SMEM)
    vmem = pl.BlockSpec(memory_space=pltpu.VMEM)
    return pl.pallas_call(
        functools.partial(gradient_kernel, ends),
        out_shape=(
            jax.ShapeDtypeStruct((2, rows, width), jnp.bfloat16),
            jax.ShapeDtypeStruct((1, 1), jnp.float32),
        ),
        in_specs=[smem, smem, vmem],
        out_specs=(vmem, vmem),
        scratch_shapes=[
            pltpu.VMEM((2, rows, width), jnp.float32),
            pltpu.VMEM((8, width), jnp.float32),
        ],
        compiler_params=pltpu.CompilerParams(vmem_limit_bytes=vmem_bytes),
        cost_estimate=cost_of(60 * rows * width, 12 * rows * width),
        name="gradient",
    )(cells, coefs, wind_ext)


def y_forward(grad, component, table, slabs):
    _, rows, width = grad.shape
    part = width // slabs
    block = max(part, min(512, width))
    return pl.pallas_call(
        y_forward_kernel,
        grid=(width // block,),
        out_shape=jax.ShapeDtypeStruct((slabs, rows, part), jnp.bfloat16),
        in_specs=[
            pl.BlockSpec((1, rows, width), lambda j: (component, 0, 0)),
            pl.BlockSpec((width, block), lambda j: (0, j)),
        ],
        out_specs=pl.BlockSpec((block // part, rows, part), lambda j: (j, 0, 0)),
        compiler_params=params(1),
        cost_estimate=cost_of(2 * rows * width * width, 2 * width * (width + 2 * rows)),
        name="y_forward",
    )(grad, table)


def x_transforms(cols, table, lam_x, lam_y):
    slabs, rows, part = cols.shape
    length = slabs * rows
    block = max(rows, min(512, length))
    return pl.pallas_call(
        x_kernel,
        grid=(2, length // block),
        out_shape=(
            jax.ShapeDtypeStruct((slabs, rows, part), jnp.bfloat16),
            jax.ShapeDtypeStruct((8, part), jnp.float32),
        ),
        in_specs=[
            whole((slabs, rows, part)),
            pl.BlockSpec((block, length), lambda p, i: (i, 0)),
            pl.BlockSpec((block, 1), lambda p, i: (i, 0)),
            whole((1, part)),
        ],
        out_specs=(
            pl.BlockSpec((block // rows, rows, part), lambda p, i: (p * i, 0, 0)),
            whole((8, part)),
        ),
        scratch_shapes=[pltpu.VMEM((length, part), jnp.bfloat16)],
        compiler_params=params(2),
        cost_estimate=cost_of(4 * length * length * part, 4 * length * (length + part)),
        name="x_transforms",
    )(cols, table, lam_x, lam_y)


def y_back(rows_in, table):
    slabs, rows, part = rows_in.shape
    width = slabs * part
    block = min(512, width)
    return pl.pallas_call(
        y_back_kernel,
        grid=(width // block,),
        out_shape=jax.ShapeDtypeStruct((rows, width), jnp.float32),
        in_specs=[
            whole((slabs, rows, part)),
            pl.BlockSpec((width, block), lambda j: (0, j)),
        ],
        out_specs=pl.BlockSpec((rows, block), lambda j: (0, j)),
        scratch_shapes=[pltpu.VMEM((rows, width), jnp.bfloat16)],
        compiler_params=params(1),
        cost_estimate=cost_of(2 * rows * width * width, 2 * width * (width + 3 * rows)),
        name="y_back",
    )(rows_in, table)


def exchange(buf):
    return lax.all_to_all(buf, "slab", split_axis=0, concat_axis=0, tiled=True)


def local(wind, obs_velocity, gate_weight, azimuth, block_owner, block_cell):
    slabs = lax.axis_size("slab")
    here = lax.axis_index("slab")
    field = wind[0]
    width_x, _, width_y = field.shape
    total_x = width_x * slabs
    part_y = width_y // slabs
    blocks, _ = obs_velocity.shape
    capacity = 2 * blocks // slabs

    owner = block_owner[:, 0]
    match = (owner[:, None] == lax.iota(jnp.int32, slabs)[None, :]).astype(jnp.int32)
    before = jnp.cumsum(match, axis=0) - match
    slot = owner * capacity + jnp.sum(before * match, axis=1)
    wc = gate_weight * jnp.cos(azimuth)
    ws = gate_weight * jnp.sin(azimuth)
    coefs = jnp.stack(
        [
            jnp.sum(wc * wc, axis=1),
            jnp.sum(wc * ws, axis=1),
            jnp.sum(ws * ws, axis=1),
            jnp.sum(wc * obs_velocity, axis=1),
            jnp.sum(ws * obs_velocity, axis=1),
            block_cell.astype(jnp.float32),
        ]
    )
    cost_own = 0.5 * jnp.sum(obs_velocity * obs_velocity)
    placed = (slot[:, None] == lax.iota(jnp.int32, slabs * capacity)[None, :]).astype(jnp.float32)
    sent = jnp.dot(coefs, placed, precision=lax.Precision.HIGHEST)
    sent = sent.reshape(6, slabs, capacity).transpose(1, 0, 2)
    got = exchange(jnp.concatenate([sent, jnp.zeros((slabs, 2, capacity), jnp.float32)], axis=1))
    cells = jnp.round(got[:, 5]).astype(jnp.int32)

    ends = slabs - 1
    low = lax.ppermute(field[width_x - 2 :], "slab", [(i, i + 1) for i in range(ends)])
    high = lax.ppermute(field[:2], "slab", [(i + 1, i) for i in range(ends)])
    pad = jnp.zeros((halo - 2, 2, width_y), jnp.float32)
    wind_ext = jnp.concatenate([pad, low, field, high, pad], axis=0).transpose(1, 0, 2)

    gradient, cost_part = gradient_of(cells, got, wind_ext, width_x, total_x)

    table_y = lax.optimization_barrier(dst_table(width_y))
    table_x = table_y if total_x == width_y else lax.optimization_barrier(dst_table(total_x))
    lam_x = eigen_values(total_x, 0, total_x)[:, None]
    lam_y = eigen_values(width_y, here * part_y, part_y)[None, :]

    spectra = [exchange(y_forward(gradient, c, table_y, slabs)) for c in range(2)]
    solved = [x_transforms(cols, table_x, lam_x, lam_y) for cols in spectra]
    energy_part = jnp.sum(solved[0][1]) + jnp.sum(solved[1][1])
    sums = lax.psum(
        jnp.stack([cost_own + cost_part[0, 0], energy_part]), ("slab", "radar")
    )
    cost_total = sums[0]
    precond = [y_back(exchange(back), table_y) for back, _ in solved]
    updated = field - cost_total / sums[1] * jnp.stack(precond, axis=1)
    return (updated[None], jnp.reshape(cost_total, (1,)))


def solution(mesh):
    return jax.shard_map(
        local,
        mesh=mesh,
        in_specs=(
            P(("groups", "radar"), "slab", None, None),
            P(("groups", "slab", "radar"), None),
            P(("groups", "slab", "radar"), None),
            P(("groups", "slab", "radar"), None),
            P(("groups", "slab", "radar"), None),
            P(("groups", "slab", "radar")),
        ),
        out_specs=(P(("groups", "radar"), "slab", None, None), P("groups")),
        check_vma=False,
    )
```

```python
import functools
import math

import jax
import jax.numpy as jnp
from jax import lax
from jax.experimental import pallas as pl
from jax.experimental.pallas import tpu as pltpu
from jax.sharding import PartitionSpec as P

divergence_weight = 2.0
spectral_shift = 0.0001
vmem_bytes = 56 * 1024 * 1024
halo = 8


def dst_table(length):
    inner = math.gcd(length, 64)
    outer = length // inner
    waves = lax.iota(jnp.int32, length) + 1
    period = 2 * (length + 1)
    scale = math.sqrt(2.0 / (length + 1))

    def angles(steps):
        phase = steps[:, None] * waves[None, :] % period
        return math.pi / (length + 1) * phase.astype(jnp.float32)

    coarse = angles(lax.iota(jnp.int32, outer) * inner)
    fine = angles(lax.iota(jnp.int32, inner) + 1)
    coarse_s, coarse_c, fine_s, fine_c = lax.optimization_barrier(
        (scale * jnp.sin(coarse), scale * jnp.cos(coarse), jnp.sin(fine), jnp.cos(fine))
    )
    table = coarse_s[:, None, :] * fine_c[None] + coarse_c[:, None, :] * fine_s[None]
    return table.astype(jnp.bfloat16).reshape(length, length)


def eigen_values(length, start, count):
    waves = (start + lax.iota(jnp.int32, count) + 1).astype(jnp.float32)
    return 4.0 * jnp.sin(math.pi / (2 * (length + 1)) * waves) ** 2


def gradient_kernel(component, ends, cell_ref, coef_ref, wind_ref, low_ref, high_ref, *refs):
    out_ref, grad_ref = refs[0], refs[-1]
    rows, width = out_ref.shape
    slabs, _, capacity = coef_ref.shape
    here = lax.axis_index("slab")
    step = min(32, rows)
    count = rows // step
    tall = step + 2 * halo
    with_cost = component == 1
    if with_cost:
        cost_ref, sum_ref = refs[1], refs[2]
        sum_ref[...] = jnp.zeros_like(sum_ref)
    lane = lax.broadcasted_iota(jnp.int32, (tall, width), 1)
    row = lax.broadcasted_iota(jnp.int32, (tall, width), 0)

    def y_sides(field):
        before = jnp.where(lane == 0, 0.0, pltpu.roll(field, 1, 1))
        after = jnp.where(lane == width - 1, 0.0, pltpu.roll(field, width - 1, 1))
        return before, after

    def stencil(i, carry):
        start = pl.multiple_of(i * step, 8)
        above = pl.ds(pl.multiple_of(jnp.maximum(start - halo, 0), 8), halo)
        below = pl.ds(pl.multiple_of(jnp.minimum(start + step, rows - halo), 8), halo)

        def tall_block(c):
            return jnp.concatenate(
                [
                    jnp.where(i == 0, low_ref[c], wind_ref[c, above, :]),
                    wind_ref[c, pl.ds(start, step), :],
                    jnp.where(i == count - 1, high_ref[c], wind_ref[c, below, :]),
                ],
                axis=0,
            )

        u, v = tall_block(0), tall_block(1)
        before, after = y_sides(v)
        div = 0.5 * (pltpu.roll(u, tall - 1, 0) - pltpu.roll(u, 1, 0)) + 0.5 * (after - before)
        place = here * rows + start - halo + row
        div = jnp.where((place >= 0) & (place < ends), div, 0.0)
        if with_cost:
            kept = div[halo : halo + step]
            sum_ref[...] += jnp.sum((kept * kept).reshape(step // 8, 8, width), axis=0)
            before, after = y_sides(div)
            grad = before - after
        else:
            grad = pltpu.roll(div, 1, 0) - pltpu.roll(div, tall - 1, 0)
        grad_ref[pl.ds(start, step), :] = divergence_weight * 0.5 * grad[halo : halo + step]
        return carry

    lax.fori_loop(0, count, stencil, 0)

    spot = lax.broadcasted_iota(jnp.int32, (8, 128), 0) * 128
    spot = spot + lax.broadcasted_iota(jnp.int32, (8, 128), 1)

    def gate_block(s, i, total):
        cell = cell_ref[s, i]
        x = cell // width
        y = cell - x * width
        top = pl.multiple_of(x // 8 * 8, 8)
        first = pl.multiple_of(y // 128 * 128, 128)
        mask = spot == (x - top) * 128 + (y - first)
        u = wind_ref[0, pl.ds(top, 8), pl.ds(first, 128)]
        v = wind_ref[1, pl.ds(top, 8), pl.ds(first, 128)]
        uv = coef_ref[s, 1, i]
        if with_cost:
            uu, vv = coef_ref[s, 0, i], coef_ref[s, 2, i]
            ou, ov = coef_ref[s, 3, i], coef_ref[s, 4, i]
            part = uv * u + vv * v - ov
            total = total + jnp.where(
                mask, u * (uu * u + uv * v - 2.0 * ou) + v * (part - ov), 0.0
            )
        else:
            part = coef_ref[s, 0, i] * u + uv * v - coef_ref[s, 3, i]
        grad_ref[pl.ds(top, 8), pl.ds(first, 128)] += jnp.where(mask, part, 0.0)
        return total

    def gate_group(t, total):
        s = t // (capacity // 8)
        base = (t - s * (capacity // 8)) * 8
        for k in range(8):
            total = gate_block(s, base + k, total)
        return total

    total = lax.fori_loop(
        0, slabs * capacity // 8, gate_group, jnp.zeros((8, 128), jnp.float32)
    )
    if with_cost:
        cost_div = 0.5 * divergence_weight * jnp.sum(sum_ref[...], keepdims=True)
        cost_ref[...] = cost_div + 0.5 * jnp.sum(total, keepdims=True)

    def lower(i, carry):
        at = pl.ds(pl.multiple_of(i * step, 16), step)
        out_ref[at, :] = grad_ref[at, :].astype(jnp.bfloat16)
        return carry

    lax.fori_loop(0, count, lower, 0)


def y_forward_kernel(grad_ref, table_ref, out_ref):
    parts, _, part = out_ref.shape
    spec = jnp.dot(grad_ref[...], table_ref[...], preferred_element_type=jnp.float32)
    spec = spec.astype(jnp.bfloat16)
    for d in range(parts):
        out_ref[d] = spec[:, d * part : (d + 1) * part]


def x_kernel(cols_ref, table_ref, lam_x_ref, lam_y_ref, out_ref, energy_ref, scaled_ref):
    phase, i = pl.program_id(0), pl.program_id(1)
    slabs, rows, part = cols_ref.shape
    block = table_ref.shape[0]

    @pl.when((phase == 0) & (i == 0))
    def _():
        energy_ref[...] = jnp.zeros_like(energy_ref)

    @pl.when(phase == 0)
    def _():
        cols = cols_ref[...].reshape(slabs * rows, part)
        spec = jnp.dot(table_ref[...], cols, preferred_element_type=jnp.float32)
        scaled = spec / (lam_x_ref[...] + lam_y_ref[...] + spectral_shift)
        energy_ref[...] += jnp.sum((spec * scaled).reshape(block // 8, 8, part), axis=0)
        scaled_ref[pl.ds(pl.multiple_of(i * block, block), block), :] = scaled.astype(jnp.bfloat16)

    @pl.when(phase == 1)
    def _():
        back = jnp.dot(table_ref[...], scaled_ref[...], preferred_element_type=jnp.float32)
        out_ref[...] = back.astype(jnp.bfloat16).reshape(out_ref.shape)


def y_back_kernel(rows_ref, table_ref, out_ref, held_ref):
    slabs, _, part = rows_ref.shape

    @pl.when(pl.program_id(0) == 0)
    def _():
        for d in range(slabs):
            held_ref[:, d * part : (d + 1) * part] = rows_ref[d]

    out_ref[...] = jnp.dot(held_ref[...], table_ref[...], preferred_element_type=jnp.float32)


def whole(shape):
    return pl.BlockSpec(shape, lambda *_: (0,) * len(shape))


def cost_of(flops, moved):
    return pl.CostEstimate(flops=flops, bytes_accessed=moved, transcendentals=0)


def params(steps):
    return pltpu.CompilerParams(
        vmem_limit_bytes=vmem_bytes, dimension_semantics=("arbitrary",) * steps
    )


def gradient_of(component, cells, coefs, field, low, high, ends):
    _, rows, width = field.shape
    smem = pl.BlockSpec(memory_space=pltpu.SMEM)
    vmem = pl.BlockSpec(memory_space=pltpu.VMEM)
    out_shape = [jax.ShapeDtypeStruct((rows, width), jnp.bfloat16)]
    scratch = [pltpu.VMEM((rows, width), jnp.float32)]
    if component == 1:
        out_shape.append(jax.ShapeDtypeStruct((1, 1), jnp.float32))
        scratch.insert(0, pltpu.VMEM((8, width), jnp.float32))
    return pl.pallas_call(
        functools.partial(gradient_kernel, component, ends),
        out_shape=out_shape,
        in_specs=[smem, smem, vmem, vmem, vmem],
        out_specs=[vmem] * len(out_shape),
        scratch_shapes=scratch,
        compiler_params=pltpu.CompilerParams(vmem_limit_bytes=vmem_bytes),
        cost_estimate=cost_of(60 * rows * width, 12 * rows * width),
        name="gradient_" + "uv"[component],
    )(cells, coefs, field, low, high)


def y_forward(grad, table, slabs):
    rows, width = grad.shape
    part = width // slabs
    block = max(part, min(512, width))
    return pl.pallas_call(
        y_forward_kernel,
        grid=(width // block,),
        out_shape=jax.ShapeDtypeStruct((slabs, rows, part), jnp.bfloat16),
        in_specs=[
            whole((rows, width)),
            pl.BlockSpec((width, block), lambda j: (0, j)),
        ],
        out_specs=pl.BlockSpec((block // part, rows, part), lambda j: (j, 0, 0)),
        compiler_params=params(1),
        cost_estimate=cost_of(2 * rows * width * width, 2 * width * (width + 2 * rows)),
        name="y_forward",
    )(grad, table)


def x_transforms(cols, table, lam_x, lam_y):
    slabs, rows, part = cols.shape
    length = slabs * rows
    block = max(rows, min(512, length))
    return pl.pallas_call(
        x_kernel,
        grid=(2, length // block),
        out_shape=(
            jax.ShapeDtypeStruct((slabs, rows, part), jnp.bfloat16),
            jax.ShapeDtypeStruct((8, part), jnp.float32),
        ),
        in_specs=[
            whole((slabs, rows, part)),
            pl.BlockSpec((block, length), lambda p, i: (i, 0)),
            pl.BlockSpec((block, 1), lambda p, i: (i, 0)),
            whole((1, part)),
        ],
        out_specs=(
            pl.BlockSpec((block // rows, rows, part), lambda p, i: (p * i, 0, 0)),
            whole((8, part)),
        ),
        scratch_shapes=[pltpu.VMEM((length, part), jnp.bfloat16)],
        compiler_params=params(2),
        cost_estimate=cost_of(4 * length * length * part, 4 * length * (length + part)),
        name="x_transforms",
    )(cols, table, lam_x, lam_y)


def y_back(rows_in, table):
    slabs, rows, part = rows_in.shape
    width = slabs * part
    block = min(512, width)
    return pl.pallas_call(
        y_back_kernel,
        grid=(width // block,),
        out_shape=jax.ShapeDtypeStruct((rows, width), jnp.float32),
        in_specs=[
            whole((slabs, rows, part)),
            pl.BlockSpec((width, block), lambda j: (0, j)),
        ],
        out_specs=pl.BlockSpec((rows, block), lambda j: (0, j)),
        scratch_shapes=[pltpu.VMEM((rows, width), jnp.bfloat16)],
        compiler_params=params(1),
        cost_estimate=cost_of(2 * rows * width * width, 2 * width * (width + 3 * rows)),
        name="y_back",
    )(rows_in, table)


def last_kernel(step_ref, rows_ref, table_ref, other_ref, wind_ref, out_ref, held_ref, pre_ref):
    slabs, rows, part = rows_ref.shape
    step = step_ref[0]
    some = min(32, rows)

    @pl.when(pl.program_id(0) == 0)
    def _():
        for d in range(slabs):
            held_ref[:, d * part : (d + 1) * part] = rows_ref[d]

    pre_ref[...] = jnp.dot(held_ref[...], table_ref[...], preferred_element_type=jnp.float32)

    def update(i, carry):
        at = pl.ds(pl.multiple_of(i * some, some), some)
        out_ref[at, 0, :] = wind_ref[at, 0, :] - step * other_ref[at, :]
        out_ref[at, 1, :] = wind_ref[at, 1, :] - step * pre_ref[at, :]
        return carry

    lax.fori_loop(0, rows // some, update, 0)


def last(step, rows_in, table, other, field):
    slabs, rows, part = rows_in.shape
    width = slabs * part
    block = min(512, width)
    return pl.pallas_call(
        last_kernel,
        grid=(width // block,),
        out_shape=jax.ShapeDtypeStruct((rows, 2, width), jnp.float32),
        in_specs=[
            pl.BlockSpec(memory_space=pltpu.SMEM),
            whole((slabs, rows, part)),
            pl.BlockSpec((width, block), lambda j: (0, j)),
            pl.BlockSpec((rows, block), lambda j: (0, j)),
            pl.BlockSpec((rows, 2, block), lambda j: (0, 0, j)),
        ],
        out_specs=pl.BlockSpec((rows, 2, block), lambda j: (0, 0, j)),
        scratch_shapes=[
            pltpu.VMEM((rows, width), jnp.bfloat16),
            pltpu.VMEM((rows, block), jnp.float32),
        ],
        compiler_params=params(1),
        cost_estimate=cost_of(2 * rows * width * width, 2 * width * (width + 11 * rows)),
        name="last",
    )(step, rows_in, table, other, field)


def sum_kernel(radars, own_ref, out_ref, slots, send_sem, recv_sem):
    count = slots.shape[0]
    me = lax.axis_index("slab") * radars + lax.axis_index("radar")

    def peer(k):
        other = lax.rem(me + k, count)
        return {"slab": other // radars, "radar": lax.rem(other, radars)}

    def came(k):
        return lax.rem(me + count - k, count)

    def copy(k, slot):
        return pltpu.make_async_remote_copy(
            src_ref=own_ref,
            dst_ref=slots.at[slot],
            send_sem=send_sem.at[k],
            recv_sem=recv_sem.at[slot],
            device_id=peer(k),
            device_id_type=pl.DeviceIdType.MESH,
        )

    barrier = pltpu.get_barrier_semaphore()

    def greet(k, carry):
        pl.semaphore_signal(
            barrier, inc=1, device_id=peer(k), device_id_type=pl.DeviceIdType.MESH
        )
        return carry

    def send(k, carry):
        copy(k, me).start()
        return carry

    def finish(k, carry):
        copy(k, me).wait_send()
        copy(k, came(k)).wait_recv()
        return carry

    lax.fori_loop(1, count, greet, 0)
    pl.semaphore_wait(barrier, count - 1)
    lax.fori_loop(1, count, send, 0)
    slots[me] = own_ref[...]
    lax.fori_loop(1, count, finish, 0)
    out_ref[...] = jnp.sum(slots[...], axis=0)


def summed(own, slabs, radars):
    count = slabs * radars
    return pl.pallas_call(
        functools.partial(sum_kernel, radars),
        out_shape=jax.ShapeDtypeStruct(own.shape, jnp.float32),
        in_specs=[pl.BlockSpec(memory_space=pltpu.VMEM)],
        out_specs=pl.BlockSpec(memory_space=pltpu.VMEM),
        scratch_shapes=[
            pltpu.VMEM((count,) + own.shape, jnp.float32),
            pltpu.SemaphoreType.DMA((count,)),
            pltpu.SemaphoreType.DMA((count,)),
        ],
        compiler_params=pltpu.CompilerParams(collective_id=0, has_side_effects=True),
        name="summed",
    )(own)


def exchange(buf):
    return lax.all_to_all(buf, "slab", split_axis=0, concat_axis=0, tiled=True)


def local(wind, obs_velocity, gate_weight, azimuth, block_owner, block_cell):
    slabs = lax.axis_size("slab")
    here = lax.axis_index("slab")
    field = wind[0]
    width_x, _, width_y = field.shape
    total_x = width_x * slabs
    part_y = width_y // slabs
    blocks, _ = obs_velocity.shape
    capacity = 2 * blocks // slabs

    owner = block_owner[:, 0]
    match = (owner[:, None] == lax.iota(jnp.int32, slabs)[None, :]).astype(jnp.int32)
    before = jnp.cumsum(match, axis=0) - match
    slot = owner * capacity + jnp.sum(before * match, axis=1)
    wc = gate_weight * jnp.cos(azimuth)
    ws = gate_weight * jnp.sin(azimuth)
    coefs = jnp.stack(
        [
            jnp.sum(wc * wc, axis=1),
            jnp.sum(wc * ws, axis=1),
            jnp.sum(ws * ws, axis=1),
            jnp.sum(wc * obs_velocity, axis=1),
            jnp.sum(ws * obs_velocity, axis=1),
            block_cell.astype(jnp.float32),
        ]
    )
    cost_own = 0.5 * jnp.sum(obs_velocity * obs_velocity)
    placed = (slot[:, None] == lax.iota(jnp.int32, slabs * capacity)[None, :]).astype(jnp.float32)
    sent = jnp.dot(coefs, placed, precision=lax.Precision.HIGHEST)
    sent = sent.reshape(6, slabs, capacity).transpose(1, 0, 2)
    got = exchange(jnp.concatenate([sent, jnp.zeros((slabs, 2, capacity), jnp.float32)], axis=1))
    cells = jnp.round(got[:, 5]).astype(jnp.int32)

    ends = slabs - 1
    low = lax.ppermute(field[width_x - 2 :], "slab", [(i, i + 1) for i in range(ends)])
    high = lax.ppermute(field[:2], "slab", [(i + 1, i) for i in range(ends)])
    pad = jnp.zeros((halo - 2, 2, width_y), jnp.float32)
    low = jnp.concatenate([pad, low], axis=0).transpose(1, 0, 2)
    high = jnp.concatenate([high, pad], axis=0).transpose(1, 0, 2)
    apart = lax.optimization_barrier(field.transpose(1, 0, 2))
    grad_u = gradient_of(0, cells, got, apart, low, high, total_x)[0]
    table_y = lax.optimization_barrier(dst_table(width_y))
    table_x = table_y if total_x == width_y else lax.optimization_barrier(dst_table(total_x))
    lam_x = eigen_values(total_x, 0, total_x)[:, None]
    lam_y = eigen_values(width_y, here * part_y, part_y)[None, :]

    spec_u, cells_v = lax.optimization_barrier((y_forward(grad_u, table_y, slabs), cells))
    grad_v, cost_part = gradient_of(1, cells_v, got, apart, low, high, total_x)
    spectra = [exchange(spec_u), exchange(y_forward(grad_v, table_y, slabs))]
    solved = [x_transforms(cols, table_x, lam_x, lam_y) for cols in spectra]
    energy_part = jnp.sum(solved[0][1]) + jnp.sum(solved[1][1])
    lane = lax.broadcasted_iota(jnp.int32, (8, 128), 1)
    own = jnp.where(lane == 0, cost_own + cost_part[0, 0], energy_part)
    sums = summed(own, slabs, lax.axis_size("radar"))
    cost_total = sums[0, 0]
    step = jnp.reshape(cost_total / sums[0, 1], (1,))
    rows_u, rows_v = exchange(solved[0][0]), exchange(solved[1][0])
    updated = last(step, rows_v, table_y, y_back(rows_u, table_y), field)
    return (updated[None], jnp.reshape(cost_total, (1,)))


def solution(mesh):
    return jax.shard_map(
        local,
        mesh=mesh,
        in_specs=(
            P(("groups", "radar"), "slab", None, None),
            P(("groups", "slab", "radar"), None),
            P(("groups", "slab", "radar"), None),
            P(("groups", "slab", "radar"), None),
            P(("groups", "slab", "radar"), None),
            P(("groups", "slab", "radar")),
        ),
        out_specs=(P(("groups", "radar"), "slab", None, None), P("groups")),
        check_vma=False,
    )
```

```python
import functools
import math

import jax
import jax.numpy as jnp
from jax import lax
from jax.experimental import pallas as pl
from jax.experimental.pallas import tpu as pltpu
from jax.sharding import PartitionSpec as P

divergence_weight = 2.0
spectral_shift = 0.0001
vmem_bytes = 56 * 1024 * 1024
halo = 8


def dst_table(length):
    inner = math.gcd(length, 64)
    outer = length // inner
    waves = lax.iota(jnp.int32, length) + 1
    period = 2 * (length + 1)
    scale = math.sqrt(2.0 / (length + 1))

    def angles(steps):
        phase = steps[:, None] * waves[None, :] % period
        return math.pi / (length + 1) * phase.astype(jnp.float32)

    coarse = angles(lax.iota(jnp.int32, outer) * inner)
    fine = angles(lax.iota(jnp.int32, inner) + 1)
    coarse_s, coarse_c, fine_s, fine_c = lax.optimization_barrier(
        (scale * jnp.sin(coarse), scale * jnp.cos(coarse), jnp.sin(fine), jnp.cos(fine))
    )
    table = coarse_s[:, None, :] * fine_c[None] + coarse_c[:, None, :] * fine_s[None]
    return table.astype(jnp.bfloat16).reshape(length, length)


def eigen_values(length, start, count):
    waves = (start + lax.iota(jnp.int32, count) + 1).astype(jnp.float32)
    return 4.0 * jnp.sin(math.pi / (2 * (length + 1)) * waves) ** 2


def gradient_kernel(component, ends, cell_ref, coef_ref, wind_ref, low_ref, high_ref, *refs):
    out_ref, grad_ref, apart_ref = refs[0], refs[-2], refs[-1]
    rows, width = out_ref.shape
    slabs, _, capacity = coef_ref.shape
    here = lax.axis_index("slab")
    step = min(32, rows)
    count = rows // step
    tall = step + 2 * halo
    with_cost = component == 1
    if with_cost:
        cost_ref, sum_ref = refs[1], refs[2]
        sum_ref[...] = jnp.zeros_like(sum_ref)
    lane = lax.broadcasted_iota(jnp.int32, (tall, width), 1)
    row = lax.broadcasted_iota(jnp.int32, (tall, width), 0)

    def y_sides(field):
        before = jnp.where(lane == 0, 0.0, pltpu.roll(field, 1, 1))
        after = jnp.where(lane == width - 1, 0.0, pltpu.roll(field, width - 1, 1))
        return before, after

    def stencil(i, carry):
        start = pl.multiple_of(i * step, 8)
        above = pl.ds(pl.multiple_of(jnp.maximum(start - halo, 0), 8), halo)
        below = pl.ds(pl.multiple_of(jnp.minimum(start + step, rows - halo), 8), halo)

        def tall_block(c):
            middle = wind_ref[pl.ds(start, step), c, :]
            apart_ref[c, pl.ds(start, step), :] = middle
            return jnp.concatenate(
                [
                    jnp.where(i == 0, low_ref[c], wind_ref[above, c, :]),
                    middle,
                    jnp.where(i == count - 1, high_ref[c], wind_ref[below, c, :]),
                ],
                axis=0,
            )

        u, v = tall_block(0), tall_block(1)
        before, after = y_sides(v)
        div = 0.5 * (pltpu.roll(u, tall - 1, 0) - pltpu.roll(u, 1, 0)) + 0.5 * (after - before)
        place = here * rows + start - halo + row
        div = jnp.where((place >= 0) & (place < ends), div, 0.0)
        if with_cost:
            kept = div[halo : halo + step]
            sum_ref[...] += jnp.sum((kept * kept).reshape(step // 8, 8, width), axis=0)
            before, after = y_sides(div)
            grad = before - after
        else:
            grad = pltpu.roll(div, 1, 0) - pltpu.roll(div, tall - 1, 0)
        grad_ref[pl.ds(start, step), :] = divergence_weight * 0.5 * grad[halo : halo + step]
        return carry

    lax.fori_loop(0, count, stencil, 0)

    spot = lax.broadcasted_iota(jnp.int32, (8, 128), 0) * 128
    spot = spot + lax.broadcasted_iota(jnp.int32, (8, 128), 1)

    def gate_block(s, i, total):
        top = pl.multiple_of(cell_ref[s, 0, i], 8)
        first = pl.multiple_of(cell_ref[s, 1, i], 128)
        mask = spot == cell_ref[s, 2, i]
        u = apart_ref[0, pl.ds(top, 8), pl.ds(first, 128)]
        v = apart_ref[1, pl.ds(top, 8), pl.ds(first, 128)]
        uv = coef_ref[s, 1, i]
        if with_cost:
            uu, vv = coef_ref[s, 0, i], coef_ref[s, 2, i]
            ou, ov = coef_ref[s, 3, i], coef_ref[s, 4, i]
            part = uv * u + vv * v - ov
            total = total + jnp.where(
                mask, u * (uu * u + uv * v - 2.0 * ou) + v * (part - ov), 0.0
            )
        else:
            part = coef_ref[s, 0, i] * u + uv * v - coef_ref[s, 3, i]
        grad_ref[pl.ds(top, 8), pl.ds(first, 128)] += jnp.where(mask, part, 0.0)
        return total

    def gate_group(s, t, total):
        for k in range(8):
            total = gate_block(s, t * 8 + k, total)
        return total

    def gate_slab(s, total):
        return lax.fori_loop(0, capacity // 8, functools.partial(gate_group, s), total)

    total = lax.fori_loop(0, slabs, gate_slab, jnp.zeros((8, 128), jnp.float32))
    if with_cost:
        cost_div = 0.5 * divergence_weight * jnp.sum(sum_ref[...], keepdims=True)
        cost_ref[...] = cost_div + 0.5 * jnp.sum(total, keepdims=True)

    def lower(i, carry):
        at = pl.ds(pl.multiple_of(i * step, 16), step)
        out_ref[at, :] = grad_ref[at, :].astype(jnp.bfloat16)
        return carry

    lax.fori_loop(0, count, lower, 0)


def y_forward_kernel(grad_ref, table_ref, out_ref):
    parts, _, part = out_ref.shape
    spec = jnp.dot(grad_ref[...], table_ref[...], preferred_element_type=jnp.float32)
    spec = spec.astype(jnp.bfloat16)
    for d in range(parts):
        out_ref[d] = spec[:, d * part : (d + 1) * part]


def x_kernel(cols_ref, table_ref, lam_x_ref, lam_y_ref, out_ref, energy_ref, scaled_ref):
    phase, i = pl.program_id(0), pl.program_id(1)
    slabs, rows, part = cols_ref.shape
    block = table_ref.shape[0]

    @pl.when((phase == 0) & (i == 0))
    def _():
        energy_ref[...] = jnp.zeros_like(energy_ref)

    @pl.when(phase == 0)
    def _():
        cols = cols_ref[...].reshape(slabs * rows, part)
        spec = jnp.dot(table_ref[...], cols, preferred_element_type=jnp.float32)
        scaled = spec / (lam_x_ref[...] + lam_y_ref[...] + spectral_shift)
        energy_ref[...] += jnp.sum((spec * scaled).reshape(block // 8, 8, part), axis=0)
        scaled_ref[pl.ds(pl.multiple_of(i * block, block), block), :] = scaled.astype(jnp.bfloat16)

    @pl.when(phase == 1)
    def _():
        back = jnp.dot(table_ref[...], scaled_ref[...], preferred_element_type=jnp.float32)
        out_ref[...] = back.astype(jnp.bfloat16).reshape(out_ref.shape)


def y_back_kernel(rows_ref, table_ref, out_ref, held_ref):
    slabs, _, part = rows_ref.shape

    @pl.when(pl.program_id(0) == 0)
    def _():
        for d in range(slabs):
            held_ref[:, d * part : (d + 1) * part] = rows_ref[d]

    out_ref[...] = jnp.dot(held_ref[...], table_ref[...], preferred_element_type=jnp.float32)


def whole(shape):
    return pl.BlockSpec(shape, lambda *_: (0,) * len(shape))


def cost_of(flops, moved):
    return pl.CostEstimate(flops=flops, bytes_accessed=moved, transcendentals=0)


def params(steps):
    return pltpu.CompilerParams(
        vmem_limit_bytes=vmem_bytes, dimension_semantics=("arbitrary",) * steps
    )


def gradient_of(component, cells, coefs, field, low, high, ends):
    rows, _, width = field.shape
    smem = pl.BlockSpec(memory_space=pltpu.SMEM)
    vmem = pl.BlockSpec(memory_space=pltpu.VMEM)
    out_shape = [jax.ShapeDtypeStruct((rows, width), jnp.bfloat16)]
    scratch = [
        pltpu.VMEM((rows, width), jnp.float32),
        pltpu.VMEM((2, rows, width), jnp.float32),
    ]
    if component == 1:
        out_shape.append(jax.ShapeDtypeStruct((1, 1), jnp.float32))
        scratch.insert(0, pltpu.VMEM((8, width), jnp.float32))
    return pl.pallas_call(
        functools.partial(gradient_kernel, component, ends),
        out_shape=out_shape,
        in_specs=[smem, smem, vmem, vmem, vmem],
        out_specs=[vmem] * len(out_shape),
        scratch_shapes=scratch,
        compiler_params=pltpu.CompilerParams(vmem_limit_bytes=vmem_bytes),
        cost_estimate=cost_of(60 * rows * width, 12 * rows * width),
        name="gradient_" + "uv"[component],
    )(cells, coefs, field, low, high)


def y_forward(grad, table, slabs):
    rows, width = grad.shape
    part = width // slabs
    block = max(part, min(512, width))
    return pl.pallas_call(
        y_forward_kernel,
        grid=(width // block,),
        out_shape=jax.ShapeDtypeStruct((slabs, rows, part), jnp.bfloat16),
        in_specs=[
            whole((rows, width)),
            pl.BlockSpec((width, block), lambda j: (0, j)),
        ],
        out_specs=pl.BlockSpec((block // part, rows, part), lambda j: (j, 0, 0)),
        compiler_params=params(1),
        cost_estimate=cost_of(2 * rows * width * width, 2 * width * (width + 2 * rows)),
        name="y_forward",
    )(grad, table)


def x_transforms(cols, table, lam_x, lam_y):
    slabs, rows, part = cols.shape
    length = slabs * rows
    block = max(rows, min(512, length))
    return pl.pallas_call(
        x_kernel,
        grid=(2, length // block),
        out_shape=(
            jax.ShapeDtypeStruct((slabs, rows, part), jnp.bfloat16),
            jax.ShapeDtypeStruct((8, part), jnp.float32),
        ),
        in_specs=[
            whole((slabs, rows, part)),
            pl.BlockSpec((block, length), lambda p, i: (i, 0)),
            pl.BlockSpec((block, 1), lambda p, i: (i, 0)),
            whole((1, part)),
        ],
        out_specs=(
            pl.BlockSpec((block // rows, rows, part), lambda p, i: (p * i, 0, 0)),
            whole((8, part)),
        ),
        scratch_shapes=[pltpu.VMEM((length, part), jnp.bfloat16)],
        compiler_params=params(2),
        cost_estimate=cost_of(4 * length * length * part, 4 * length * (length + part)),
        name="x_transforms",
    )(cols, table, lam_x, lam_y)


def y_back(rows_in, table):
    slabs, rows, part = rows_in.shape
    width = slabs * part
    block = min(512, width)
    return pl.pallas_call(
        y_back_kernel,
        grid=(width // block,),
        out_shape=jax.ShapeDtypeStruct((rows, width), jnp.float32),
        in_specs=[
            whole((slabs, rows, part)),
            pl.BlockSpec((width, block), lambda j: (0, j)),
        ],
        out_specs=pl.BlockSpec((rows, block), lambda j: (0, j)),
        scratch_shapes=[pltpu.VMEM((rows, width), jnp.bfloat16)],
        compiler_params=params(1),
        cost_estimate=cost_of(2 * rows * width * width, 2 * width * (width + 3 * rows)),
        name="y_back",
    )(rows_in, table)


def last_kernel(step_ref, rows_ref, table_ref, other_ref, wind_ref, out_ref, held_ref, pre_ref):
    slabs, rows, part = rows_ref.shape
    step = step_ref[0]
    some = min(32, rows)

    @pl.when(pl.program_id(0) == 0)
    def _():
        for d in range(slabs):
            held_ref[:, d * part : (d + 1) * part] = rows_ref[d]

    pre_ref[...] = jnp.dot(held_ref[...], table_ref[...], preferred_element_type=jnp.float32)

    def update(i, carry):
        at = pl.ds(pl.multiple_of(i * some, some), some)
        out_ref[at, 0, :] = wind_ref[at, 0, :] - step * other_ref[at, :]
        out_ref[at, 1, :] = wind_ref[at, 1, :] - step * pre_ref[at, :]
        return carry

    lax.fori_loop(0, rows // some, update, 0)


def last(step, rows_in, table, other, field):
    slabs, rows, part = rows_in.shape
    width = slabs * part
    block = min(512, width)
    return pl.pallas_call(
        last_kernel,
        grid=(width // block,),
        out_shape=jax.ShapeDtypeStruct((rows, 2, width), jnp.float32),
        in_specs=[
            pl.BlockSpec(memory_space=pltpu.SMEM),
            whole((slabs, rows, part)),
            pl.BlockSpec((width, block), lambda j: (0, j)),
            pl.BlockSpec((rows, block), lambda j: (0, j)),
            pl.BlockSpec((rows, 2, block), lambda j: (0, 0, j)),
        ],
        out_specs=pl.BlockSpec((rows, 2, block), lambda j: (0, 0, j)),
        scratch_shapes=[
            pltpu.VMEM((rows, width), jnp.bfloat16),
            pltpu.VMEM((rows, block), jnp.float32),
        ],
        compiler_params=params(1),
        cost_estimate=cost_of(2 * rows * width * width, 2 * width * (width + 11 * rows)),
        name="last",
    )(step, rows_in, table, other, field)


def sum_kernel(radars, own_ref, out_ref, slots, send_sem, recv_sem):
    count = slots.shape[0]
    me = lax.axis_index("slab") * radars + lax.axis_index("radar")

    def peer(k):
        other = lax.rem(me + k, count)
        return {"slab": other // radars, "radar": lax.rem(other, radars)}

    def came(k):
        return lax.rem(me + count - k, count)

    def copy(k, slot):
        return pltpu.make_async_remote_copy(
            src_ref=own_ref,
            dst_ref=slots.at[slot],
            send_sem=send_sem.at[k],
            recv_sem=recv_sem.at[slot],
            device_id=peer(k),
            device_id_type=pl.DeviceIdType.MESH,
        )

    barrier = pltpu.get_barrier_semaphore()

    def greet(k, carry):
        pl.semaphore_signal(
            barrier, inc=1, device_id=peer(k), device_id_type=pl.DeviceIdType.MESH
        )
        return carry

    def send(k, carry):
        copy(k, me).start()
        return carry

    def finish(k, carry):
        copy(k, me).wait_send()
        copy(k, came(k)).wait_recv()
        return carry

    lax.fori_loop(1, count, greet, 0)
    pl.semaphore_wait(barrier, count - 1)
    lax.fori_loop(1, count, send, 0)
    slots[me] = own_ref[...]
    lax.fori_loop(1, count, finish, 0)
    out_ref[...] = jnp.sum(slots[...], axis=0)


def summed(own, slabs, radars):
    count = slabs * radars
    return pl.pallas_call(
        functools.partial(sum_kernel, radars),
        out_shape=jax.ShapeDtypeStruct(own.shape, jnp.float32),
        in_specs=[pl.BlockSpec(memory_space=pltpu.VMEM)],
        out_specs=pl.BlockSpec(memory_space=pltpu.VMEM),
        scratch_shapes=[
            pltpu.VMEM((count,) + own.shape, jnp.float32),
            pltpu.SemaphoreType.DMA((count,)),
            pltpu.SemaphoreType.DMA((count,)),
        ],
        compiler_params=pltpu.CompilerParams(collective_id=0, has_side_effects=True),
        name="summed",
    )(own)


def exchange(buf):
    return lax.all_to_all(buf, "slab", split_axis=0, concat_axis=0, tiled=True)


def local(wind, obs_velocity, gate_weight, azimuth, block_owner, block_cell):
    slabs = lax.axis_size("slab")
    here = lax.axis_index("slab")
    field = wind[0]
    width_x, _, width_y = field.shape
    total_x = width_x * slabs
    part_y = width_y // slabs
    blocks, _ = obs_velocity.shape
    capacity = 2 * blocks // slabs

    owner = block_owner[:, 0]
    match = (owner[:, None] == lax.iota(jnp.int32, slabs)[None, :]).astype(jnp.int32)
    before = jnp.cumsum(match, axis=0) - match
    slot = owner * capacity + jnp.sum(before * match, axis=1)
    wc = gate_weight * jnp.cos(azimuth)
    ws = gate_weight * jnp.sin(azimuth)
    coefs = jnp.stack(
        [
            jnp.sum(wc * wc, axis=1),
            jnp.sum(wc * ws, axis=1),
            jnp.sum(ws * ws, axis=1),
            jnp.sum(wc * obs_velocity, axis=1),
            jnp.sum(ws * obs_velocity, axis=1),
            block_cell.astype(jnp.float32),
        ]
    )
    cost_own = 0.5 * jnp.sum(obs_velocity * obs_velocity)
    placed = (slot[:, None] == lax.iota(jnp.int32, slabs * capacity)[None, :]).astype(jnp.float32)
    sent = jnp.dot(coefs, placed, precision=lax.Precision.HIGHEST)
    sent = sent.reshape(6, slabs, capacity).transpose(1, 0, 2)
    got = exchange(jnp.concatenate([sent, jnp.zeros((slabs, 2, capacity), jnp.float32)], axis=1))
    cells = jnp.round(got[:, 5]).astype(jnp.int32)
    x, y = cells // width_y, cells % width_y
    cells = jnp.stack([x // 8 * 8, y // 128 * 128, x % 8 * 128 + y % 128], axis=1)

    ends = slabs - 1
    low = lax.ppermute(field[width_x - 2 :], "slab", [(i, i + 1) for i in range(ends)])
    high = lax.ppermute(field[:2], "slab", [(i + 1, i) for i in range(ends)])
    pad = jnp.zeros((halo - 2, 2, width_y), jnp.float32)
    low = jnp.concatenate([pad, low], axis=0).transpose(1, 0, 2)
    high = jnp.concatenate([high, pad], axis=0).transpose(1, 0, 2)
    grad_u = gradient_of(0, cells, got, field, low, high, total_x)[0]
    table_y = lax.optimization_barrier(dst_table(width_y))
    table_x = table_y if total_x == width_y else lax.optimization_barrier(dst_table(total_x))
    lam_x = eigen_values(total_x, 0, total_x)[:, None]
    lam_y = eigen_values(width_y, here * part_y, part_y)[None, :]

    spec_u, cells_v = lax.optimization_barrier((y_forward(grad_u, table_y, slabs), cells))
    grad_v, cost_part = gradient_of(1, cells_v, got, field, low, high, total_x)
    spectra = [exchange(spec_u), exchange(y_forward(grad_v, table_y, slabs))]
    solved = [x_transforms(cols, table_x, lam_x, lam_y) for cols in spectra]
    energy_part = jnp.sum(solved[0][1]) + jnp.sum(solved[1][1])
    lane = lax.broadcasted_iota(jnp.int32, (8, 128), 1)
    own = jnp.where(lane == 0, cost_own + cost_part[0, 0], energy_part)
    rows_u, own = lax.optimization_barrier((exchange(solved[0][0]), own))
    sums = summed(own, slabs, lax.axis_size("radar"))
    cost_total = sums[0, 0]
    step = jnp.reshape(cost_total / sums[0, 1], (1,))
    back_v, step = lax.optimization_barrier((solved[1][0], step))
    rows_v = exchange(back_v)
    updated = last(step, rows_v, table_y, y_back(rows_u, table_y), field)
    return (updated[None], jnp.reshape(cost_total, (1,)))


def solution(mesh):
    return jax.shard_map(
        local,
        mesh=mesh,
        in_specs=(
            P(("groups", "radar"), "slab", None, None),
            P(("groups", "slab", "radar"), None),
            P(("groups", "slab", "radar"), None),
            P(("groups", "slab", "radar"), None),
            P(("groups", "slab", "radar"), None),
            P(("groups", "slab", "radar")),
        ),
        out_specs=(P(("groups", "radar"), "slab", None, None), P("groups")),
        check_vma=False,
    )
```

```python
import functools
import math

import jax
import jax.numpy as jnp
from jax import lax
from jax.experimental import pallas as pl
from jax.experimental.pallas import tpu as pltpu
from jax.sharding import PartitionSpec as P

divergence_weight = 2.0
spectral_shift = 0.0001
vmem_bytes = 56 * 1024 * 1024
halo = 8


def dst_factors(length):
    inner = math.gcd(length, 64)
    outer = length // inner
    waves = lax.iota(jnp.int32, length) + 1
    period = 2 * (length + 1)
    scale = math.sqrt(2.0 / (length + 1))

    def angles(steps):
        phase = steps[:, None] * waves[None, :] % period
        return math.pi / (length + 1) * phase.astype(jnp.float32)

    coarse = angles(lax.iota(jnp.int32, outer) * inner)
    fine = angles(lax.iota(jnp.int32, inner) + 1)
    coarse_s, coarse_c, fine_s, fine_c = lax.optimization_barrier(
        (scale * jnp.sin(coarse), scale * jnp.cos(coarse), jnp.sin(fine), jnp.cos(fine))
    )
    return coarse_s, coarse_c, fine_s, fine_c


def dst_table(length):
    coarse_s, coarse_c, fine_s, fine_c = dst_factors(length)
    table = coarse_s[:, None, :] * fine_c[None] + coarse_c[:, None, :] * fine_s[None]
    return table.astype(jnp.bfloat16).reshape(length, length)


def eigen_values(length, start, count):
    waves = (start + lax.iota(jnp.int32, count) + 1).astype(jnp.float32)
    return 4.0 * jnp.sin(math.pi / (2 * (length + 1)) * waves) ** 2


def gradient_kernel(component, ends, cell_ref, coef_ref, wind_ref, low_ref, high_ref, *refs):
    out_ref, grad_ref, apart_ref = refs[0], refs[-2], refs[-1]
    rows, width = out_ref.shape
    slabs, _, capacity = coef_ref.shape
    here = lax.axis_index("slab")
    step = min(32, rows)
    count = rows // step
    tall = step + 2 * halo
    with_cost = component == 1
    if with_cost:
        cost_ref, sum_ref = refs[1], refs[2]
        sum_ref[...] = jnp.zeros_like(sum_ref)
    lane = lax.broadcasted_iota(jnp.int32, (tall, width), 1)
    row = lax.broadcasted_iota(jnp.int32, (tall, width), 0)

    def y_sides(field):
        before = jnp.where(lane == 0, 0.0, pltpu.roll(field, 1, 1))
        after = jnp.where(lane == width - 1, 0.0, pltpu.roll(field, width - 1, 1))
        return before, after

    def stencil(i, carry):
        start = pl.multiple_of(i * step, 8)
        above = pl.ds(pl.multiple_of(jnp.maximum(start - halo, 0), 8), halo)
        below = pl.ds(pl.multiple_of(jnp.minimum(start + step, rows - halo), 8), halo)

        def tall_block(c):
            middle = wind_ref[pl.ds(start, step), c, :]
            apart_ref[c, pl.ds(start, step), :] = middle
            return jnp.concatenate(
                [
                    jnp.where(i == 0, low_ref[c], wind_ref[above, c, :]),
                    middle,
                    jnp.where(i == count - 1, high_ref[c], wind_ref[below, c, :]),
                ],
                axis=0,
            )

        u, v = tall_block(0), tall_block(1)
        before, after = y_sides(v)
        div = 0.5 * (pltpu.roll(u, tall - 1, 0) - pltpu.roll(u, 1, 0)) + 0.5 * (after - before)
        place = here * rows + start - halo + row
        div = jnp.where((place >= 0) & (place < ends), div, 0.0)
        if with_cost:
            kept = div[halo : halo + step]
            sum_ref[...] += jnp.sum((kept * kept).reshape(step // 8, 8, width), axis=0)
            before, after = y_sides(div)
            grad = before - after
        else:
            grad = pltpu.roll(div, 1, 0) - pltpu.roll(div, tall - 1, 0)
        grad_ref[pl.ds(start, step), :] = divergence_weight * 0.5 * grad[halo : halo + step]
        return carry

    lax.fori_loop(0, count, stencil, 0)

    spot = lax.broadcasted_iota(jnp.int32, (8, 128), 0) * 128
    spot = spot + lax.broadcasted_iota(jnp.int32, (8, 128), 1)

    def gate_block(s, i, total):
        top = pl.multiple_of(cell_ref[s, 0, i], 8)
        first = pl.multiple_of(cell_ref[s, 1, i], 128)
        mask = spot == cell_ref[s, 2, i]
        u = apart_ref[0, pl.ds(top, 8), pl.ds(first, 128)]
        v = apart_ref[1, pl.ds(top, 8), pl.ds(first, 128)]
        uv = coef_ref[s, 1, i]
        if with_cost:
            uu, vv = coef_ref[s, 0, i], coef_ref[s, 2, i]
            ou, ov = coef_ref[s, 3, i], coef_ref[s, 4, i]
            part = uv * u + vv * v - ov
            total = total + jnp.where(
                mask, u * (uu * u + uv * v - 2.0 * ou) + v * (part - ov), 0.0
            )
        else:
            part = coef_ref[s, 0, i] * u + uv * v - coef_ref[s, 3, i]
        grad_ref[pl.ds(top, 8), pl.ds(first, 128)] += jnp.where(mask, part, 0.0)
        return total

    def gate_group(s, t, total):
        for k in range(8):
            total = gate_block(s, t * 8 + k, total)
        return total

    def gate_slab(s, total):
        return lax.fori_loop(0, capacity // 8, functools.partial(gate_group, s), total)

    total = lax.fori_loop(0, slabs, gate_slab, jnp.zeros((8, 128), jnp.float32))
    if with_cost:
        cost_div = 0.5 * divergence_weight * jnp.sum(sum_ref[...], keepdims=True)
        cost_ref[...] = cost_div + 0.5 * jnp.sum(total, keepdims=True)

    def lower(i, carry):
        at = pl.ds(pl.multiple_of(i * step, 16), step)
        out_ref[at, :] = grad_ref[at, :].astype(jnp.bfloat16)
        return carry

    lax.fori_loop(0, count, lower, 0)


def y_forward_kernel(grad_ref, table_ref, out_ref):
    parts, _, part = out_ref.shape
    spec = jnp.dot(grad_ref[...], table_ref[...], preferred_element_type=jnp.float32)
    spec = spec.astype(jnp.bfloat16)
    for d in range(parts):
        out_ref[d] = spec[:, d * part : (d + 1) * part]


def x_kernel(cols_ref, table_ref, lam_x_ref, lam_y_ref, out_ref, energy_ref, scaled_ref):
    phase, i = pl.program_id(0), pl.program_id(1)
    slabs, rows, part = cols_ref.shape
    block = table_ref.shape[0]

    @pl.when((phase == 0) & (i == 0))
    def _():
        energy_ref[...] = jnp.zeros_like(energy_ref)

    @pl.when(phase == 0)
    def _():
        cols = cols_ref[...].reshape(slabs * rows, part)
        spec = jnp.dot(table_ref[...], cols, preferred_element_type=jnp.float32)
        scaled = spec / (lam_x_ref[...] + lam_y_ref[...] + spectral_shift)
        energy_ref[...] += jnp.sum((spec * scaled).reshape(block // 8, 8, part), axis=0)
        scaled_ref[pl.ds(pl.multiple_of(i * block, block), block), :] = scaled.astype(jnp.bfloat16)

    @pl.when(phase == 1)
    def _():
        back = jnp.dot(table_ref[...], scaled_ref[...], preferred_element_type=jnp.float32)
        out_ref[...] = back.astype(jnp.bfloat16).reshape(out_ref.shape)


def y_back_kernel(rows_ref, table_ref, out_ref, held_ref):
    slabs, _, part = rows_ref.shape

    @pl.when(pl.program_id(0) == 0)
    def _():
        for d in range(slabs):
            held_ref[:, d * part : (d + 1) * part] = rows_ref[d]

    out_ref[...] = jnp.dot(held_ref[...], table_ref[...], preferred_element_type=jnp.float32)


def whole(shape):
    return pl.BlockSpec(shape, lambda *_: (0,) * len(shape))


def cost_of(flops, moved):
    return pl.CostEstimate(flops=flops, bytes_accessed=moved, transcendentals=0)


def params(steps):
    return pltpu.CompilerParams(
        vmem_limit_bytes=vmem_bytes, dimension_semantics=("arbitrary",) * steps
    )


def gradient_of(component, cells, coefs, field, low, high, ends):
    rows, _, width = field.shape
    smem = pl.BlockSpec(memory_space=pltpu.SMEM)
    vmem = pl.BlockSpec(memory_space=pltpu.VMEM)
    out_shape = [jax.ShapeDtypeStruct((rows, width), jnp.bfloat16)]
    scratch = [
        pltpu.VMEM((rows, width), jnp.float32),
        pltpu.VMEM((2, rows, width), jnp.float32),
    ]
    if component == 1:
        out_shape.append(jax.ShapeDtypeStruct((1, 1), jnp.float32))
        scratch.insert(0, pltpu.VMEM((8, width), jnp.float32))
    return pl.pallas_call(
        functools.partial(gradient_kernel, component, ends),
        out_shape=out_shape,
        in_specs=[smem, smem, vmem, vmem, vmem],
        out_specs=[vmem] * len(out_shape),
        scratch_shapes=scratch,
        compiler_params=pltpu.CompilerParams(vmem_limit_bytes=vmem_bytes),
        cost_estimate=cost_of(60 * rows * width, 12 * rows * width),
        name="gradient_" + "uv"[component],
    )(cells, coefs, field, low, high)


def y_first_kernel(grad_ref, cs_ref, cc_ref, fs_ref, fc_ref, out_ref, table_ref):
    inner = fs_ref.shape[0]
    for a in range(cs_ref.shape[0]):
        rows = cs_ref[a : a + 1] * fc_ref[...] + cc_ref[a : a + 1] * fs_ref[...]
        table_ref[a * inner : (a + 1) * inner, :] = rows.astype(jnp.bfloat16)
    y_forward_kernel(grad_ref, table_ref, out_ref)


def y_first(grad, slabs):
    rows, width = grad.shape
    part = width // slabs
    block = max(part, min(512, width))
    factors = dst_factors(width)
    return pl.pallas_call(
        y_first_kernel,
        grid=(width // block,),
        out_shape=(
            jax.ShapeDtypeStruct((slabs, rows, part), jnp.bfloat16),
            jax.ShapeDtypeStruct((width, width), jnp.bfloat16),
        ),
        in_specs=[whole((rows, width))]
        + [pl.BlockSpec((f.shape[0], block), lambda j: (0, j)) for f in factors],
        out_specs=(
            pl.BlockSpec((block // part, rows, part), lambda j: (j, 0, 0)),
            pl.BlockSpec((width, block), lambda j: (0, j)),
        ),
        compiler_params=params(1),
        cost_estimate=cost_of(2 * rows * width * width, 2 * width * (width + 2 * rows)),
        name="y_first",
    )(grad, *factors)


def y_forward(grad, table, slabs):
    rows, width = grad.shape
    part = width // slabs
    block = max(part, min(512, width))
    return pl.pallas_call(
        y_forward_kernel,
        grid=(width // block,),
        out_shape=jax.ShapeDtypeStruct((slabs, rows, part), jnp.bfloat16),
        in_specs=[
            whole((rows, width)),
            pl.BlockSpec((width, block), lambda j: (0, j)),
        ],
        out_specs=pl.BlockSpec((block // part, rows, part), lambda j: (j, 0, 0)),
        compiler_params=params(1),
        cost_estimate=cost_of(2 * rows * width * width, 2 * width * (width + 2 * rows)),
        name="y_forward",
    )(grad, table)


def x_transforms(cols, table, lam_x, lam_y):
    slabs, rows, part = cols.shape
    length = slabs * rows
    block = max(rows, min(512, length))
    return pl.pallas_call(
        x_kernel,
        grid=(2, length // block),
        out_shape=(
            jax.ShapeDtypeStruct((slabs, rows, part), jnp.bfloat16),
            jax.ShapeDtypeStruct((8, part), jnp.float32),
        ),
        in_specs=[
            whole((slabs, rows, part)),
            pl.BlockSpec((block, length), lambda p, i: (i, 0)),
            pl.BlockSpec((block, 1), lambda p, i: (i, 0)),
            whole((1, part)),
        ],
        out_specs=(
            pl.BlockSpec((block // rows, rows, part), lambda p, i: (p * i, 0, 0)),
            whole((8, part)),
        ),
        scratch_shapes=[pltpu.VMEM((length, part), jnp.bfloat16)],
        compiler_params=params(2),
        cost_estimate=cost_of(4 * length * length * part, 4 * length * (length + part)),
        name="x_transforms",
    )(cols, table, lam_x, lam_y)


def y_back(rows_in, table):
    slabs, rows, part = rows_in.shape
    width = slabs * part
    block = min(512, width)
    return pl.pallas_call(
        y_back_kernel,
        grid=(width // block,),
        out_shape=jax.ShapeDtypeStruct((rows, width), jnp.float32),
        in_specs=[
            whole((slabs, rows, part)),
            pl.BlockSpec((width, block), lambda j: (0, j)),
        ],
        out_specs=pl.BlockSpec((rows, block), lambda j: (0, j)),
        scratch_shapes=[pltpu.VMEM((rows, width), jnp.bfloat16)],
        compiler_params=params(1),
        cost_estimate=cost_of(2 * rows * width * width, 2 * width * (width + 3 * rows)),
        name="y_back",
    )(rows_in, table)


def last_kernel(step_ref, rows_ref, table_ref, other_ref, wind_ref, out_ref, held_ref, pre_ref):
    slabs, rows, part = rows_ref.shape
    step = step_ref[0]
    some = min(32, rows)

    @pl.when(pl.program_id(0) == 0)
    def _():
        for d in range(slabs):
            held_ref[:, d * part : (d + 1) * part] = rows_ref[d]

    pre_ref[...] = jnp.dot(held_ref[...], table_ref[...], preferred_element_type=jnp.float32)

    def update(i, carry):
        at = pl.ds(pl.multiple_of(i * some, some), some)
        out_ref[at, 0, :] = wind_ref[at, 0, :] - step * other_ref[at, :]
        out_ref[at, 1, :] = wind_ref[at, 1, :] - step * pre_ref[at, :]
        return carry

    lax.fori_loop(0, rows // some, update, 0)


def last(step, rows_in, table, other, field):
    slabs, rows, part = rows_in.shape
    width = slabs * part
    block = min(512, width)
    return pl.pallas_call(
        last_kernel,
        grid=(width // block,),
        out_shape=jax.ShapeDtypeStruct((rows, 2, width), jnp.float32),
        in_specs=[
            pl.BlockSpec(memory_space=pltpu.SMEM),
            whole((slabs, rows, part)),
            pl.BlockSpec((width, block), lambda j: (0, j)),
            pl.BlockSpec((rows, block), lambda j: (0, j)),
            pl.BlockSpec((rows, 2, block), lambda j: (0, 0, j)),
        ],
        out_specs=pl.BlockSpec((rows, 2, block), lambda j: (0, 0, j)),
        scratch_shapes=[
            pltpu.VMEM((rows, width), jnp.bfloat16),
            pltpu.VMEM((rows, block), jnp.float32),
        ],
        compiler_params=params(1),
        cost_estimate=cost_of(2 * rows * width * width, 2 * width * (width + 11 * rows)),
        name="last",
    )(step, rows_in, table, other, field)


def sum_kernel(radars, own_ref, out_ref, slots, send_sem, recv_sem):
    count = slots.shape[0]
    me = lax.axis_index("slab") * radars + lax.axis_index("radar")

    def peer(k):
        other = lax.rem(me + k, count)
        return {"slab": other // radars, "radar": lax.rem(other, radars)}

    def came(k):
        return lax.rem(me + count - k, count)

    def copy(k, slot):
        return pltpu.make_async_remote_copy(
            src_ref=own_ref,
            dst_ref=slots.at[slot],
            send_sem=send_sem.at[k],
            recv_sem=recv_sem.at[slot],
            device_id=peer(k),
            device_id_type=pl.DeviceIdType.MESH,
        )

    barrier = pltpu.get_barrier_semaphore()

    def greet(k, carry):
        pl.semaphore_signal(
            barrier, inc=1, device_id=peer(k), device_id_type=pl.DeviceIdType.MESH
        )
        return carry

    def send(k, carry):
        copy(k, me).start()
        return carry

    def finish(k, carry):
        copy(k, me).wait_send()
        copy(k, came(k)).wait_recv()
        return carry

    lax.fori_loop(1, count, greet, 0)
    pl.semaphore_wait(barrier, count - 1)
    lax.fori_loop(1, count, send, 0)
    slots[me] = own_ref[...]
    lax.fori_loop(1, count, finish, 0)
    out_ref[...] = jnp.sum(slots[...], axis=0)


def summed(own, slabs, radars):
    count = slabs * radars
    return pl.pallas_call(
        functools.partial(sum_kernel, radars),
        out_shape=jax.ShapeDtypeStruct(own.shape, jnp.float32),
        in_specs=[pl.BlockSpec(memory_space=pltpu.VMEM)],
        out_specs=pl.BlockSpec(memory_space=pltpu.VMEM),
        scratch_shapes=[
            pltpu.VMEM((count,) + own.shape, jnp.float32),
            pltpu.SemaphoreType.DMA((count,)),
            pltpu.SemaphoreType.DMA((count,)),
        ],
        compiler_params=pltpu.CompilerParams(collective_id=0, has_side_effects=True),
        name="summed",
    )(own)


def exchange(buf):
    return lax.all_to_all(buf, "slab", split_axis=0, concat_axis=0, tiled=True)


def local(wind, obs_velocity, gate_weight, azimuth, block_owner, block_cell):
    slabs = lax.axis_size("slab")
    here = lax.axis_index("slab")
    field = wind[0]
    width_x, _, width_y = field.shape
    total_x = width_x * slabs
    part_y = width_y // slabs
    blocks, _ = obs_velocity.shape
    capacity = 2 * blocks // slabs

    owner = block_owner[:, 0]
    match = (owner[:, None] == lax.iota(jnp.int32, slabs)[None, :]).astype(jnp.int32)
    before = jnp.cumsum(match, axis=0) - match
    slot = owner * capacity + jnp.sum(before * match, axis=1)
    wc = gate_weight * jnp.cos(azimuth)
    ws = gate_weight * jnp.sin(azimuth)
    coefs = jnp.stack(
        [
            jnp.sum(wc * wc, axis=1),
            jnp.sum(wc * ws, axis=1),
            jnp.sum(ws * ws, axis=1),
            jnp.sum(wc * obs_velocity, axis=1),
            jnp.sum(ws * obs_velocity, axis=1),
            block_cell.astype(jnp.float32),
        ]
    )
    cost_own = 0.5 * jnp.sum(obs_velocity * obs_velocity)
    placed = (slot[:, None] == lax.iota(jnp.int32, slabs * capacity)[None, :]).astype(jnp.float32)
    sent = jnp.dot(coefs, placed, precision=lax.Precision.HIGHEST)
    sent = sent.reshape(6, slabs, capacity).transpose(1, 0, 2)
    got = exchange(jnp.concatenate([sent, jnp.zeros((slabs, 2, capacity), jnp.float32)], axis=1))
    cells = jnp.round(got[:, 5]).astype(jnp.int32)
    x, y = cells // width_y, cells % width_y
    cells = jnp.stack([x // 8 * 8, y // 128 * 128, x % 8 * 128 + y % 128], axis=1)

    ends = slabs - 1
    low = lax.ppermute(field[width_x - 2 :], "slab", [(i, i + 1) for i in range(ends)])
    high = lax.ppermute(field[:2], "slab", [(i + 1, i) for i in range(ends)])
    pad = jnp.zeros((halo - 2, 2, width_y), jnp.float32)
    low = jnp.concatenate([pad, low], axis=0).transpose(1, 0, 2)
    high = jnp.concatenate([high, pad], axis=0).transpose(1, 0, 2)
    grad_u = gradient_of(0, cells, got, field, low, high, total_x)[0]
    spec_u, table_y = y_first(grad_u, slabs)
    table_x = table_y if total_x == width_y else lax.optimization_barrier(dst_table(total_x))
    lam_x = eigen_values(total_x, 0, total_x)[:, None]
    lam_y = eigen_values(width_y, here * part_y, part_y)[None, :]

    spec_u, cells_v = lax.optimization_barrier((spec_u, cells))
    grad_v, cost_part = gradient_of(1, cells_v, got, field, low, high, total_x)
    spec_v = y_forward(grad_v, table_y, slabs)
    cols_u, _ = lax.optimization_barrier((exchange(spec_u), spec_v))
    spectra = [cols_u, exchange(spec_v)]
    solved = [x_transforms(cols, table_x, lam_x, lam_y) for cols in spectra]
    energy_part = jnp.sum(solved[0][1]) + jnp.sum(solved[1][1])
    lane = lax.broadcasted_iota(jnp.int32, (8, 128), 1)
    own = jnp.where(lane == 0, cost_own + cost_part[0, 0], energy_part)
    pre_u, own = lax.optimization_barrier((y_back(exchange(solved[0][0]), table_y), own))
    rows_v = exchange(solved[1][0])
    sums = summed(own, slabs, lax.axis_size("radar"))
    cost_total = sums[0, 0]
    step = jnp.reshape(cost_total / sums[0, 1], (1,))
    updated = last(step, rows_v, table_y, pre_u, field)
    return (updated[None], jnp.reshape(cost_total, (1,)))


def solution(mesh):
    return jax.shard_map(
        local,
        mesh=mesh,
        in_specs=(
            P(("groups", "radar"), "slab", None, None),
            P(("groups", "slab", "radar"), None),
            P(("groups", "slab", "radar"), None),
            P(("groups", "slab", "radar"), None),
            P(("groups", "slab", "radar"), None),
            P(("groups", "slab", "radar")),
        ),
        out_specs=(P(("groups", "radar"), "slab", None, None), P("groups")),
        check_vma=False,
    )
```
